32 devices in a mesh: gx: 2 (over y), gy: 4 (over z), gz: 4 (over x, core).
Axes of the slice: x: 2, y: 2, z: 4, core: 2. Of those that a mesh axis runs over, the one named last changes fastest.
Arguments:
- inputs: bfloat16 [32, 8, 64, 512], P(None, 'gx', 'gy', 'gz'), may hold values from -6 to 6
- pre_first: bfloat16 [32, 8, 64, 512], P(None, 'gx', 'gy', 'gz'), may hold values from -6 to 6
- pre_second: bfloat16 [32, 8, 64, 512], P(None, 'gx', 'gy', 'gz'), may hold values from -6 to 6
- cotangent: bfloat16 [32, 8, 64, 512], P(None, 'gx', 'gy', 'gz'), may hold values from -6 to 6
- weight_first: bfloat16 [27, 32, 32], replicated, may hold values from -0.21875 to 0.21875
- weight_second: bfloat16 [27, 32, 32], replicated, may hold values from -0.21875 to 0.21875
Outputs:
- grad_inputs: bfloat16 [32, 8, 64, 512], P(None, 'gx', 'gy', 'gz')
- grad_first: float32 [27, 32, 32], replicated
- grad_second: float32 [27, 32, 32], replicated
The draws below stay inside these ranges and needn't reach their ends.
All inputs are finite; a program needn't handle non-finite values.
Results may differ from the reference program's by a relative error of at most 0.005.
Values may be sent and summed in bfloat16 or wider, within the bound.
A program may use at most 128 MiB of HBM per device.

```python
import math
import jax
import jax.numpy as jnp
from jax import lax

CH = 32
NX = 8
NY = 64
NZ = 512


def levels(own_key, shape, pieces, low, top_value):
    def one(position, shards_of):
        steps = jax.random.uniform(jax.random.fold_in(jax.random.fold_in(own_key, 6), position), (shards_of,), jnp.float32, low / len(pieces), top_value / len(pieces))
        return jnp.repeat(jnp.exp(steps), shape[position] // shards_of).reshape((-1,) + (1,) * (len(shape) - position - 1))

    loudness = one(*pieces[0])
    for cut in pieces[1:]:
        loudness = loudness * one(*cut)
    return loudness


def noise(stream_key, shape, width, reach, cuts=(), kind=jnp.bfloat16):
    drawn = jax.random.normal(stream_key, shape, jnp.float32) * width
    if len(cuts) > 0:
        drawn = levels(stream_key, shape, cuts, -0.22, 0.18) * drawn
    return jnp.clip(drawn, min=-reach, max=reach).astype(kind)


def setup_inputs(seed: int = 0) -> dict:
    keys = jax.random.split(jax.random.key(seed), 7)
    return {
        "inputs": noise(keys[0], (CH, NX, NY, NZ), 1.0, 6.0, ((1, 2), (2, 4), (3, 4))),
        "pre_first": noise(keys[1], (CH, NX, NY, NZ), 1.0, 6.0, ((1, 2), (2, 4), (3, 4))),
        "pre_second": noise(keys[2], (CH, NX, NY, NZ), 1.0, 6.0, ((1, 2), (2, 4), (3, 4))),
        "cotangent": noise(keys[3], (CH, NX, NY, NZ), 1.0, 6.0, ((1, 2), (2, 4), (3, 4))),
        "weight_first": noise(keys[4], (27, CH, CH), (27 * CH) ** -0.5, 0.21875),
        "weight_second": noise(keys[5], (27, CH, CH), (27 * CH) ** -0.5, 0.21875),
    }


def convolve(volume, weight):
    kernel = weight.reshape(3, 3, 3, weight.shape[1], weight.shape[2])
    return lax.conv_general_dilated(volume[None], kernel, (1, 1, 1), [(1, 1), (1, 1), (1, 1)], dimension_numbers=('NCDHW', 'DHWIO', 'NCDHW'), precision=lax.Precision.HIGHEST)[0]

def reference(inputs, pre_first, pre_second, cotangent, weight_first, weight_second):
    scale = 1.0 / math.sqrt(NX * NY * NZ)
    active = jnp.maximum(pre_first, jnp.zeros_like(pre_first))
    delta_two = jnp.where(pre_second > 0, cotangent, jnp.zeros_like(cotangent))
    unused, backward_two = jax.vjp(convolve, active.astype(jnp.float32), weight_second.astype(jnp.float32))
    back_two, grad_second = backward_two(delta_two.astype(jnp.float32))
    delta_one = jnp.where(pre_first > 0, back_two, jnp.zeros_like(back_two)).astype(jnp.bfloat16)
    unused_one, backward_one = jax.vjp(convolve, inputs.astype(jnp.float32), weight_first.astype(jnp.float32))
    back_one, grad_first = backward_one(delta_one.astype(jnp.float32))
    return (back_one.astype(jnp.bfloat16), grad_first * scale, grad_second * scale)
```

```python
import math

import jax
import jax.numpy as jnp
from jax import lax
from jax.experimental import pallas as pl
from jax.experimental.pallas import tpu as pltpu
from jax.sharding import PartitionSpec as P

MESH = pl.DeviceIdType.MESH
BF = jnp.bfloat16
F32 = jnp.float32


def exchange(k, e, faces_out, faces_in, send, recv):
    rows, _, cols, ch, nz = e.shape
    flat = cols * ch

    def axis_stage(axis, slot, up_src, up_dst, down_src, down_dst):
        me, n = lax.axis_index(axis), lax.axis_size(axis)
        has_up, has_down = me < n - 1, me > 0
        up = pltpu.make_async_remote_copy(
            up_src, up_dst, send.at[k, slot], recv.at[k, slot],
            device_id={axis: jnp.minimum(me + 1, n - 1)}, device_id_type=MESH)
        down = pltpu.make_async_remote_copy(
            down_src, down_dst, send.at[k, slot + 1], recv.at[k, slot + 1],
            device_id={axis: jnp.maximum(me - 1, 0)}, device_id_type=MESH)

        def start():
            @pl.when(has_up)
            def _():
                up.start()

            @pl.when(has_down)
            def _():
                down.start()

            @pl.when(jnp.logical_not(has_down))
            def _():
                up_dst[...] = jnp.zeros(up_dst.shape, up_dst.dtype)

            @pl.when(jnp.logical_not(has_up))
            def _():
                down_dst[...] = jnp.zeros(down_dst.shape, down_dst.dtype)

        def wait():
            @pl.when(has_up)
            def _():
                up.wait_send()
                down.wait_recv()

            @pl.when(has_down)
            def _():
                down.wait_send()
                up.wait_recv()

        return start, wait

    inner = pl.ds(1, rows - 2)
    x_start, x_wait = axis_stage(
        "gx", 0, e.at[inner, 1, cols - 2], e.at[inner, 1, 0],
        e.at[inner, 1, 1], e.at[inner, 1, cols - 1])
    y_start, y_wait = axis_stage(
        "gy", 2, e.at[rows - 2, 1], e.at[0, 1], e.at[1, 1], e.at[rows - 1, 1])
    z_start, z_wait = axis_stage(
        "gz", 4, faces_out.at[k, 0], faces_in.at[k, 0],
        faces_out.at[k, 1], faces_in.at[k, 1])

    def pack():
        r = lax.broadcasted_iota(jnp.int32, (64, nz), 0)
        lane = lax.broadcasted_iota(jnp.int32, (64, nz), 1)

        def step(y, total):
            pick = ((r == y) & (lane == nz - 1)) | ((r == y + 32) & (lane == 0))
            plane = e[y, 1].reshape(flat, nz)
            return total + lax.dot_general(
                jnp.where(pick, 1.0, 0.0).astype(BF), plane,
                (((1,), (1,)), ((), ())), preferred_element_type=F32)

        total = lax.fori_loop(0, rows, step, jnp.zeros((64, flat), F32))
        faces_out[k, 0] = total[:32].astype(BF)
        faces_out[k, 1] = total[32:].astype(BF)

    def unpack():
        kk = lax.broadcasted_iota(jnp.int32, (2 * nz, 2 * nz), 0)
        nn = lax.broadcasted_iota(jnp.int32, (2 * nz, 2 * nz), 1)
        own = kk < nz
        left = (nn < nz) & ((own & (kk == nn - 1))
                            | ((nn == 0) & (kk >= nz) & (kk < nz + 32)))
        right = (nn >= nz) & ((own & (kk == nn - nz + 1))
                              | ((nn == 2 * nz - 1) & (kk >= nz + 32) & (kk < nz + 64)))
        shift = jnp.where(left | right, 1.0, 0.0).astype(BF)
        got = jnp.concatenate([faces_in[k, 0], faces_in[k, 1]], 0).astype(F32)
        got = jnp.concatenate([got, jnp.zeros((nz - 64, flat), F32)], 0)
        got = jnp.concatenate([got, jnp.zeros((nz, 256 - flat), F32)], 1)
        columns = got.T[:flat]
        lane = lax.broadcasted_iota(jnp.int32, (flat, nz), 1)

        def step(y, _):
            mine = jnp.where((lane == y) | (lane == y + 32), columns, 0.0).astype(BF)
            plane = e[y, 1].reshape(flat, nz)
            out = jnp.dot(jnp.concatenate([plane, mine], 1), shift,
                          preferred_element_type=F32).astype(BF)
            e[y, 0] = out[:, :nz].reshape(cols, ch, nz)
            e[y, 2] = out[:, nz:].reshape(cols, ch, nz)
            return 0

        lax.fori_loop(0, rows, step, 0)

    return x_start, x_wait, y_start, y_wait, pack, z_start, z_wait, unpack


def banded(t_ref, w_ref, nx):
    ch = w_ref.shape[1]
    t_ref[...] = jnp.zeros(t_ref.shape, BF)
    for x in range(nx):
        for tap in range(27):
            ra, rb, rc = 2 - tap // 9, 2 - tap // 3 % 3, 2 - tap % 3
            col = ((rb * 3 + rc) * (nx + 2) + x + ra) * ch
            t_ref[x * ch:(x + 1) * ch, col:col + ch] = w_ref[tap]


def pair(e, y):
    _, three, cols, ch, nz = e.shape
    depth = 3 * three * cols * ch
    return jnp.concatenate([e[pl.ds(y, 3)].reshape(depth, nz),
                            e[pl.ds(y + 1, 3)].reshape(depth, nz)], 1)


def conv(e, t_ref, sink):
    ny, nz = e.shape[0] - 2, e.shape[-1]

    def step(j, _):
        y = 2 * j
        out = jnp.dot(t_ref[...], pair(e, y), preferred_element_type=F32)
        sink(y, out[:, :nz])
        sink(y + 1, out[:, nz:])
        return 0

    lax.fori_loop(0, ny // 2, step, 0)


def gram(e, a_ref, relu, acc, out_ref, which):
    ny, nx, ch, nz = a_ref.shape
    acc[...] = jnp.zeros(acc.shape, F32)

    def step(j, _):
        y = 2 * j
        a = jnp.concatenate([a_ref[y].reshape(nx * ch, nz), a_ref[y + 1].reshape(nx * ch, nz)], 1)
        if relu:
            a = jnp.maximum(a, jnp.zeros_like(a))
        acc[...] += lax.dot_general(a, pair(e, y), (((1,), (1,)), ((), ())),
                                    preferred_element_type=F32)
        return 0

    lax.fori_loop(0, ny // 2, step, 0)
    for m in range(9):
        base = m * (nx + 2) * ch
        total = acc[0:ch, base:base + 3 * ch]
        for x in range(1, nx):
            total = total + acc[x * ch:(x + 1) * ch, base + x * ch:base + (x + 3) * ch]
        out_ref[which, m, :, :3 * ch] = total
        out_ref[which, m, :, 3 * ch:] = jnp.zeros((ch, 128 - 3 * ch), F32)


def kernel(d2, p1, inp, w1, w2, gin, grads, e2, e1, t2, t1, acc, faces_out, faces_in, send, recv):
    ny, nx, ch, nz = d2.shape
    barrier = pltpu.get_barrier_semaphore()
    for axis in ("gx", "gy", "gz"):
        me, n = lax.axis_index(axis), lax.axis_size(axis)

        @pl.when(me > 0)
        def _():
            pl.semaphore_signal(barrier, inc=1, device_id={axis: jnp.maximum(me - 1, 0)},
                                device_id_type=MESH)

        @pl.when(me < n - 1)
        def _():
            pl.semaphore_signal(barrier, inc=1, device_id={axis: jnp.minimum(me + 1, n - 1)},
                                device_id_type=MESH)

    e2[pl.ds(1, ny), 1, pl.ds(1, nx)] = d2[...]
    neighbours = 0
    for axis in ("gx", "gy", "gz"):
        me, n = lax.axis_index(axis), lax.axis_size(axis)
        neighbours = neighbours + (me > 0).astype(jnp.int32) + (me < n - 1).astype(jnp.int32)
    pl.semaphore_wait(barrier, neighbours)

    stages = exchange(0, e2, faces_out, faces_in, send, recv)
    x_start, x_wait, y_start, y_wait, pack, z_start, z_wait, unpack = stages
    x_start()
    banded(t2, w2, nx)
    x_wait()
    y_start()
    banded(t1, w1, nx)
    y_wait()
    pack()
    z_start()
    z_wait()
    unpack()

    def masked(y, value):
        keep = p1[y].reshape(nx * ch, nz).astype(F32) > 0
        e1[y + 1, 1, pl.ds(1, nx)] = jnp.where(keep, value, 0.0).astype(BF).reshape(nx, ch, nz)

    conv(e2, t2, masked)
    stages = exchange(1, e1, faces_out, faces_in, send, recv)
    x_start, x_wait, y_start, y_wait, pack, z_start, z_wait, unpack = stages
    x_start()
    x_wait()
    y_start()
    y_wait()
    pack()
    z_start()
    gram(e2, p1, True, acc, grads, 1)
    z_wait()
    unpack()
    gram(e1, inp, False, acc, grads, 0)

    def rounded(y, value):
        gin[y] = value.astype(BF).reshape(nx, ch, nz)

    conv(e1, t1, rounded)


def local(inputs, pre_first, pre_second, cotangent, weight_first, weight_second):
    ch, nx, ny, nz = inputs.shape
    cells = nx * ny * nz * lax.axis_size("gx") * lax.axis_size("gy") * lax.axis_size("gz")
    scale = 1.0 / math.sqrt(cells)
    order = (2, 1, 0, 3)
    delta_two = jnp.where(pre_second > 0, cotangent, jnp.zeros_like(cotangent))
    d2, p1, inp = (jnp.transpose(v, order) for v in (delta_two, pre_first, inputs))
    vmem = pl.BlockSpec(memory_space=pltpu.VMEM)
    depth = 9 * (nx + 2) * ch
    brick = (ny + 2, 3, nx + 2, ch, nz)
    gin, grads = pl.pallas_call(
        kernel,
        out_shape=(jax.ShapeDtypeStruct((ny, nx, ch, nz), BF),
                   jax.ShapeDtypeStruct((2, 9, ch, 128), F32)),
        in_specs=[vmem] * 5,
        out_specs=(vmem, vmem),
        scratch_shapes=[
            pltpu.VMEM(brick, BF),
            pltpu.VMEM(brick, BF),
            pltpu.VMEM((nx * ch, depth), BF),
            pltpu.VMEM((nx * ch, depth), BF),
            pltpu.VMEM((nx * ch, depth), F32),
            pltpu.VMEM((2, 2, 32, (nx + 2) * ch), BF),
            pltpu.VMEM((2, 2, 32, (nx + 2) * ch), BF),
            pltpu.SemaphoreType.DMA((2, 6)),
            pltpu.SemaphoreType.DMA((2, 6)),
        ],
        compiler_params=pltpu.CompilerParams(
            collective_id=0, has_side_effects=True, vmem_limit_bytes=48 * 2**20),
    )(d2, p1, inp, weight_first, weight_second)
    total = lax.psum(grads, ("gx", "gy", "gz")) * scale
    total = total[..., :3 * ch].reshape(2, 3, 3, ch, 3, ch)
    total = jnp.flip(jnp.transpose(total, (0, 4, 1, 2, 3, 5)), (1, 2, 3)).reshape(2, 27, ch, ch)
    return jnp.transpose(gin, order), total[0], total[1]


def solution(mesh):
    cells = P(None, "gx", "gy", "gz")
    return jax.shard_map(local, mesh=mesh, in_specs=(cells,) * 4 + (P(), P()),
                         out_specs=(cells, P(), P()), check_vma=False)
```

```python
import functools
import math

import jax
import jax.numpy as jnp
from jax import lax
from jax.experimental import pallas as pl
from jax.experimental.pallas import tpu as pltpu
from jax.sharding import PartitionSpec as P

MESH = pl.DeviceIdType.MESH
BF = jnp.bfloat16
F32 = jnp.float32


def exchange(k, e, faces_out, faces_in, send, recv):
    rows, _, cols, ch, nz = e.shape
    flat = cols * ch

    def axis_stage(axis, slot, up_src, up_dst, down_src, down_dst):
        me, n = lax.axis_index(axis), lax.axis_size(axis)
        has_up, has_down = me < n - 1, me > 0
        up = pltpu.make_async_remote_copy(
            up_src, up_dst, send.at[k, slot], recv.at[k, slot],
            device_id={axis: jnp.minimum(me + 1, n - 1)}, device_id_type=MESH)
        down = pltpu.make_async_remote_copy(
            down_src, down_dst, send.at[k, slot + 1], recv.at[k, slot + 1],
            device_id={axis: jnp.maximum(me - 1, 0)}, device_id_type=MESH)

        def start():
            @pl.when(has_up)
            def _():
                up.start()

            @pl.when(has_down)
            def _():
                down.start()

            @pl.when(jnp.logical_not(has_down))
            def _():
                up_dst[...] = jnp.zeros(up_dst.shape, up_dst.dtype)

            @pl.when(jnp.logical_not(has_up))
            def _():
                down_dst[...] = jnp.zeros(down_dst.shape, down_dst.dtype)

        def wait():
            @pl.when(has_up)
            def _():
                up.wait_send()
                down.wait_recv()

            @pl.when(has_down)
            def _():
                down.wait_send()
                up.wait_recv()

        return start, wait

    inner = pl.ds(1, rows - 2)
    x_start, x_wait = axis_stage(
        "gx", 0, e.at[inner, 1, cols - 2], e.at[inner, 1, 0],
        e.at[inner, 1, 1], e.at[inner, 1, cols - 1])
    y_start, y_wait = axis_stage(
        "gy", 2, e.at[rows - 2, 1], e.at[0, 1], e.at[1, 1], e.at[rows - 1, 1])
    z_start, z_wait = axis_stage(
        "gz", 4, faces_out.at[k, 0], faces_in.at[k, 0],
        faces_out.at[k, 1], faces_in.at[k, 1])

    def pack():
        r = lax.broadcasted_iota(jnp.int32, (64, nz), 0)
        lane = lax.broadcasted_iota(jnp.int32, (64, nz), 1)

        def step(y, total):
            pick = ((r == y) & (lane == nz - 1)) | ((r == y + 32) & (lane == 0))
            plane = e[y, 1].reshape(flat, nz)
            return total + lax.dot_general(
                jnp.where(pick, 1.0, 0.0).astype(BF), plane,
                (((1,), (1,)), ((), ())), preferred_element_type=F32)

        total = lax.fori_loop(0, rows, step, jnp.zeros((64, flat), F32))
        faces_out[k, 0] = total[:32].astype(BF)
        faces_out[k, 1] = total[32:].astype(BF)

    def unpack():
        kk = lax.broadcasted_iota(jnp.int32, (2 * nz, 2 * nz), 0)
        nn = lax.broadcasted_iota(jnp.int32, (2 * nz, 2 * nz), 1)
        own = kk < nz
        left = (nn < nz) & ((own & (kk == nn - 1))
                            | ((nn == 0) & (kk >= nz) & (kk < nz + 32)))
        right = (nn >= nz) & ((own & (kk == nn - nz + 1))
                              | ((nn == 2 * nz - 1) & (kk >= nz + 32) & (kk < nz + 64)))
        shift = jnp.where(left | right, 1.0, 0.0).astype(BF)
        got = jnp.concatenate([faces_in[k, 0], faces_in[k, 1]], 0).astype(F32)
        got = jnp.concatenate([got, jnp.zeros((nz - 64, flat), F32)], 0)
        got = jnp.concatenate([got, jnp.zeros((nz, 256 - flat), F32)], 1)
        columns = got.T[:flat]
        lane = lax.broadcasted_iota(jnp.int32, (flat, nz), 1)

        def step(y, _):
            mine = jnp.where((lane == y) | (lane == y + 32), columns, 0.0).astype(BF)
            plane = e[y, 1].reshape(flat, nz)
            out = jnp.dot(jnp.concatenate([plane, mine], 1), shift,
                          preferred_element_type=F32).astype(BF)
            e[y, 0] = out[:, :nz].reshape(cols, ch, nz)
            e[y, 2] = out[:, nz:].reshape(cols, ch, nz)
            return 0

        lax.fori_loop(0, rows, step, 0)

    return x_start, x_wait, y_start, y_wait, pack, z_start, z_wait, unpack


def banded(t_ref, w_ref, nx):
    ch = w_ref.shape[1]
    t_ref[...] = jnp.zeros(t_ref.shape, BF)
    for x in range(nx):
        for tap in range(27):
            ra, rb, rc = 2 - tap // 9, 2 - tap // 3 % 3, 2 - tap % 3
            col = ((rb * 3 + rc) * (nx + 2) + x + ra) * ch
            t_ref[x * ch:(x + 1) * ch, col:col + ch] = w_ref[tap]


def pair(e, y):
    _, three, cols, ch, nz = e.shape
    depth = 3 * three * cols * ch
    return jnp.concatenate([e[pl.ds(y, 3)].reshape(depth, nz),
                            e[pl.ds(y + 1, 3)].reshape(depth, nz)], 1)


def conv(e, t_ref, sink, begin=0, end=None):
    ny, nz = e.shape[0] - 2, e.shape[-1]

    def step(j, _):
        y = 2 * j
        out = jnp.dot(t_ref[...], pair(e, y), preferred_element_type=F32)
        sink(y, out[:, :nz])
        sink(y + 1, out[:, nz:])
        return 0

    lax.fori_loop(begin, ny // 2 if end is None else end, step, 0)


def gram(e, a_ref, relu, acc, part, which):
    per = part.shape[1]
    ny, nx, ch, nz = a_ref.shape
    acc[...] = jnp.zeros(acc.shape, F32)

    def step(j, _):
        y = 2 * j
        a = jnp.concatenate([a_ref[y].reshape(nx * ch, nz), a_ref[y + 1].reshape(nx * ch, nz)], 1)
        if relu:
            a = jnp.maximum(a, jnp.zeros_like(a))
        acc[...] += lax.dot_general(a, pair(e, y), (((1,), (1,)), ((), ())),
                                    preferred_element_type=F32)
        return 0

    lax.fori_loop(0, ny // 2, step, 0)
    for m in range(9):
        base = m * (nx + 2) * ch
        total = acc[0:ch, base:base + 3 * ch]
        for x in range(1, nx):
            total = total + acc[x * ch:(x + 1) * ch, base + x * ch:base + (x + 3) * ch]
        total = jnp.concatenate([total, jnp.zeros((ch, 128 - 3 * ch), F32)], 1)
        for i in range(ch // 8):
            block = (which * 9 + m) * (ch // 8) + i
            part[block // per, block % per] = total[8 * i:8 * i + 8]


def everyone():
    ny, nz = lax.axis_size("gy"), lax.axis_size("gz")
    n = lax.axis_size("gx") * ny * nz
    me = (lax.axis_index("gx") * ny + lax.axis_index("gy")) * nz + lax.axis_index("gz")

    def place(k):
        p = (me + k) % n
        return (p // (ny * nz), p // nz % ny, p % nz)

    return n, me, place


def scatter_copy(part, got, sems, k):
    n, me, place = everyone()
    return pltpu.make_async_remote_copy(
        part.at[(me + k) % n], got.at[k], sems[0].at[k], sems[1].at[k],
        device_id=place(k), device_id_type=MESH)


def gather_copy(whole, sems, k):
    n, me, place = everyone()
    return pltpu.make_async_remote_copy(
        whole.at[me], whole.at[me], sems[2].at[k], sems[3].at[k],
        device_id=place(k), device_id_type=MESH)


def over_peers(act):
    def step(k, _):
        act(k)
        return 0

    lax.fori_loop(1, everyone()[0], step, 0)


def kernel(d2, p1, inp, w1, w2, gin, first, second, e2, e1, t2, t1, acc, faces_out, faces_in,
           part, got, whole, send, recv, *sems, scale):
    ny, nx, ch, nz = d2.shape
    n, me, place = everyone()
    barrier = pltpu.get_barrier_semaphore()

    def greet(k, _):
        pl.semaphore_signal(barrier, inc=1, device_id=place(k), device_id_type=MESH)
        return 0

    lax.fori_loop(1, n, greet, 0)
    e2[pl.ds(1, ny), 1, pl.ds(1, nx)] = d2[...]
    pl.semaphore_wait(barrier, n - 1)
    stages = exchange(0, e2, faces_out, faces_in, send, recv)
    x_start, x_wait, y_start, y_wait, pack, z_start, z_wait, unpack = stages
    x_start()
    banded(t2, w2, nx)
    x_wait()
    y_start()
    banded(t1, w1, nx)
    y_wait()
    pack()
    z_start()
    z_wait()
    unpack()

    def masked(y, value):
        keep = p1[y].reshape(nx * ch, nz).astype(F32) > 0
        e1[y + 1, 1, pl.ds(1, nx)] = jnp.where(keep, value, 0.0).astype(BF).reshape(nx, ch, nz)

    conv(e2, t2, masked)
    stages = exchange(1, e1, faces_out, faces_in, send, recv)
    x_start, x_wait, y_start, y_wait, pack, z_start, z_wait, unpack = stages
    x_start()
    x_wait()
    y_start()
    y_wait()
    pack()
    z_start()
    gram(e2, p1, True, acc, part, 1)
    z_wait()
    unpack()
    gram(e1, inp, False, acc, part, 0)

    def rounded(y, value):
        gin[y] = value.astype(BF).reshape(nx, ch, nz)

    per = part.shape[1]
    blocks = 2 * 9 * (ch // 8)
    for block in range(blocks, n * per):
        part[block // per, block % per] = jnp.zeros((8, 128), F32)
    over_peers(lambda k: scatter_copy(part, got, sems, k).start())
    conv(e1, t1, rounded, 0, ny // 4)
    over_peers(lambda k: scatter_copy(part, got, sems, k).wait())
    whole[me] = lax.fori_loop(1, n, lambda k, t: t + got[k], part[me]) * scale
    over_peers(lambda k: gather_copy(whole, sems, k).start())
    conv(e1, t1, rounded, ny // 4, ny // 2)
    over_peers(lambda k: gather_copy(whole, sems, k).wait())
    for which, out in enumerate((first, second)):
        for m in range(9):
            for i in range(ch // 8):
                block = (which * 9 + m) * (ch // 8) + i
                value = whole[block // per, block % per]
                for ra in range(3):
                    out[(2 - ra) * 9 + 8 - m, 8 * i:8 * i + 8, :] = value[:, ra * ch:(ra + 1) * ch]


def local(inputs, pre_first, pre_second, cotangent, weight_first, weight_second):
    ch, nx, ny, nz = inputs.shape
    cells = nx * ny * nz * lax.axis_size("gx") * lax.axis_size("gy") * lax.axis_size("gz")
    scale = 1.0 / math.sqrt(cells)
    order = (2, 1, 0, 3)
    delta_two = jnp.where(pre_second > 0, cotangent, jnp.zeros_like(cotangent))
    d2, p1, inp = (jnp.transpose(v, order) for v in (delta_two, pre_first, inputs))
    vmem = pl.BlockSpec(memory_space=pltpu.VMEM)
    depth = 9 * (nx + 2) * ch
    brick = (ny + 2, 3, nx + 2, ch, nz)
    n = lax.axis_size("gx") * lax.axis_size("gy") * lax.axis_size("gz")
    per = -(-(2 * 9 * ch // 8) // n)
    gin, first, second = pl.pallas_call(
        functools.partial(kernel, scale=scale),
        out_shape=(jax.ShapeDtypeStruct((ny, nx, ch, nz), BF),
                   jax.ShapeDtypeStruct(weight_first.shape, F32),
                   jax.ShapeDtypeStruct(weight_second.shape, F32)),
        in_specs=[vmem] * 5,
        out_specs=(vmem,) * 3,
        scratch_shapes=[
            pltpu.VMEM(brick, BF),
            pltpu.VMEM(brick, BF),
            pltpu.VMEM((nx * ch, depth), BF),
            pltpu.VMEM((nx * ch, depth), BF),
            pltpu.VMEM((nx * ch, depth), F32),
            pltpu.VMEM((2, 2, 32, (nx + 2) * ch), BF),
            pltpu.VMEM((2, 2, 32, (nx + 2) * ch), BF),
            pltpu.VMEM((n, per, 8, 128), F32),
            pltpu.VMEM((n, per, 8, 128), F32),
            pltpu.VMEM((n, per, 8, 128), F32),
            pltpu.SemaphoreType.DMA((2, 6)),
            pltpu.SemaphoreType.DMA((2, 6)),
        ] + [pltpu.SemaphoreType.DMA((n,))] * 4,
        compiler_params=pltpu.CompilerParams(
            collective_id=0, has_side_effects=True, vmem_limit_bytes=48 * 2**20),
    )(d2, p1, inp, weight_first, weight_second)
    return jnp.transpose(gin, order), first, second


def solution(mesh):
    cells = P(None, "gx", "gy", "gz")
    return jax.shard_map(local, mesh=mesh, in_specs=(cells,) * 4 + (P(), P()),
                         out_specs=(cells, P(), P()), check_vma=False)
```

```python
import functools
import math

import jax
import jax.numpy as jnp
from jax import lax
from jax.experimental import pallas as pl
from jax.experimental.pallas import tpu as pltpu
from jax.sharding import PartitionSpec as P

MESH = pl.DeviceIdType.MESH
BF = jnp.bfloat16
F32 = jnp.float32


DIRECTIONS = [(dx, dy, dz) for dz in (0, 1, -1) for dx in (0, 1, -1) for dy in (0, 1, -1)
              if (dx, dy, dz) != (0, 0, 0)]


def near(direction, sign):
    exists, place = None, []
    for axis, d in zip(("gx", "gy", "gz"), direction):
        me, n = lax.axis_index(axis), lax.axis_size(axis)
        if d:
            there = me + sign * d
            ok = (there >= 0) & (there < n)
            exists = ok if exists is None else exists & ok
            me = jnp.clip(there, 0, n - 1)
        place.append(me)
    return exists, tuple(place)


def clear_halo(e):
    rows, _, cols, ch, nz = e.shape
    for y in (0, rows - 1):
        e[y, 1] = jnp.zeros((cols, ch, nz), BF)
    for x in (0, cols - 1):
        e[pl.ds(1, rows - 2), 1, x] = jnp.zeros((rows - 2, ch, nz), BF)


def exchange(k, e, faces_out, faces_in, edge, send, recv):
    rows, _, cols, ch, nz = e.shape
    nx, ny, flat = cols - 2, rows - 2, cols * ch

    def ends(d, n):
        if d == 0:
            return pl.ds(1, n), pl.ds(1, n)
        return (n, 0) if d > 0 else (1, n + 1)

    def copy(i):
        dx, dy, dz = DIRECTIONS[i]
        if dz == 0:
            (sx, tx), (sy, ty) = ends(dx, nx), ends(dy, ny)
            src, dst = e.at[sy, 1, sx], e.at[ty, 1, tx]
        else:
            side = 0 if dz > 0 else 1
            src = faces_out.at[k, side]
            dst = faces_in.at[k, side, (dx + 1) * 3 + dy + 1]
        exists, place = near(DIRECTIONS[i], 1)
        return exists, pltpu.make_async_remote_copy(
            src, dst, send.at[k, i], recv.at[k, i], device_id=place, device_id_type=MESH)

    def start(picked):
        for i in picked:
            exists, one = copy(i)
            pl.when(exists)(one.start)

    def begin():
        start(range(8))
        r = lax.broadcasted_iota(jnp.int32, (2 * ny, 2 * nz), 0)
        lane = lax.broadcasted_iota(jnp.int32, (2 * ny, 2 * nz), 1)
        total = jnp.zeros((2 * ny, nx * ch), F32)
        for y in range(0, ny, 2):
            pick = (((r == y) & (lane == nz - 1)) | ((r == y + ny) & (lane == 0))
                    | ((r == y + 1) & (lane == 2 * nz - 1)) | ((r == y + 1 + ny) & (lane == nz)))
            planes = jnp.concatenate(
                [e[y + 1 + j, 1, pl.ds(1, nx)].reshape(nx * ch, nz) for j in (0, 1)], 1)
            total = total + lax.dot_general(
                jnp.where(pick, 1.0, 0.0).astype(BF), planes,
                (((1,), (1,)), ((), ())), preferred_element_type=F32)
        faces_out[k, 0] = total[:ny].astype(BF)
        faces_out[k, 1] = total[ny:].astype(BF)
        start(range(8, 26))

    def finish():
        for i in range(26):
            exists, one = copy(i)
            pl.when(exists)(one.wait_send)
            came, _ = near(DIRECTIONS[i], -1)
            pl.when(came)(one.wait_recv)

        kk = lax.broadcasted_iota(jnp.int32, (2 * nz, 2 * nz), 0)
        nn = lax.broadcasted_iota(jnp.int32, (2 * nz, 2 * nz), 1)
        own = kk < nz
        left = (nn < nz) & ((own & (kk == nn - 1))
                            | ((nn == 0) & (kk >= nz) & (kk < nz + 32)))
        right = (nn >= nz) & ((own & (kk == nn - nz + 1))
                              | ((nn == 2 * nz - 1) & (kk >= nz + 32) & (kk < nz + 64)))
        shift = jnp.where(left | right, 1.0, 0.0).astype(BF)
        for side in (0, 1):
            for dx in (-1, 0, 1):
                for dy in (-1, 0, 1):
                    face = faces_in[k, side, (dx + 1) * 3 + dy + 1].astype(F32)
                    at = 32 * side
                    if dy == 0:
                        ys, yt = slice(0, ny), slice(at + 1, at + 1 + ny)
                    elif dy > 0:
                        ys, yt = slice(ny - 1, ny), slice(at, at + 1)
                    else:
                        ys, yt = slice(0, 1), slice(at + ny + 1, at + ny + 2)
                    if dx == 0:
                        xs, xt = slice(0, nx * ch), slice(ch, ch + nx * ch)
                    elif dx > 0:
                        xs, xt = slice((nx - 1) * ch, nx * ch), slice(0, ch)
                    else:
                        xs, xt = slice(0, ch), slice((nx + 1) * ch, (nx + 2) * ch)
                    edge[yt, xt] = face[ys, xs]
        columns = edge[...].T[:flat]
        lane = lax.broadcasted_iota(jnp.int32, (flat, nz), 1)

        def step(j, _):
            y = 3 * j
            mine = jnp.concatenate(
                [jnp.where((lane == y + i) | (lane == y + i + 32), columns, 0.0).astype(BF)
                 for i in range(3)], 0)
            planes = e[pl.ds(y, 3), 1].reshape(3 * flat, nz)
            out = jnp.dot(jnp.concatenate([planes, mine], 1), shift,
                          preferred_element_type=F32).astype(BF)
            e[pl.ds(y, 3), 0] = out[:, :nz].reshape(3, cols, ch, nz)
            e[pl.ds(y, 3), 2] = out[:, nz:].reshape(3, cols, ch, nz)
            return 0

        lax.fori_loop(0, rows // 3, step, 0)

    return begin, finish


def banded(t_ref, w_ref, nx):
    ch = w_ref.shape[1]
    t_ref[...] = jnp.zeros(t_ref.shape, BF)
    for x in range(nx):
        for tap in range(27):
            ra, rb, rc = 2 - tap // 9, 2 - tap // 3 % 3, 2 - tap % 3
            col = ((rb * 3 + rc) * (nx + 2) + x + ra) * ch
            t_ref[x * ch:(x + 1) * ch, col:col + ch] = w_ref[tap]


def group(e, y):
    _, three, cols, ch, nz = e.shape
    depth = 3 * three * cols * ch
    return jnp.concatenate([e[pl.ds(y + i, 3)].reshape(depth, nz) for i in range(4)], 1)


def conv(e, t_ref, sink, begin, end):
    nz = e.shape[-1]

    def step(j, _):
        y = 4 * j
        out = jnp.dot(t_ref[...], group(e, y), preferred_element_type=F32)
        for i in range(4):
            sink(y + i, out[:, i * nz:(i + 1) * nz])
        return 0

    lax.fori_loop(begin, end, step, 0)


def gram(e, a_ref, relu, acc, part, which):
    per = part.shape[1]
    ny, nx, ch, nz = a_ref.shape
    acc[...] = jnp.zeros(acc.shape, F32)

    def step(j, _):
        y = 4 * j
        a = jnp.concatenate([a_ref[y + i].reshape(nx * ch, nz) for i in range(4)], 1)
        if relu:
            a = jnp.maximum(a, jnp.zeros_like(a))
        acc[...] += lax.dot_general(a, group(e, y), (((1,), (1,)), ((), ())),
                                    preferred_element_type=F32)
        return 0

    lax.fori_loop(0, ny // 4, step, 0)
    for m in range(9):
        base = m * (nx + 2) * ch
        total = acc[0:ch, base:base + 3 * ch]
        for x in range(1, nx):
            total = total + acc[x * ch:(x + 1) * ch, base + x * ch:base + (x + 3) * ch]
        for ra in range(3):
            q = (which * 9 + m) * 3 + ra
            lane = q % 4 * ch
            for h in range(ch // 16):
                block = q // 4 * (ch // 16) + h
                part[block // per, block % per, :, lane:lane + ch] = (
                    total[16 * h:16 * h + 16, ra * ch:(ra + 1) * ch])


def everyone():
    ny, nz = lax.axis_size("gy"), lax.axis_size("gz")
    n = lax.axis_size("gx") * ny * nz
    me = (lax.axis_index("gx") * ny + lax.axis_index("gy")) * nz + lax.axis_index("gz")

    def place(k):
        p = (me + k) % n
        return (p // (ny * nz), p // nz % ny, p % nz)

    return n, me, place


def scatter_copy(part, got, sems, k):
    n, me, place = everyone()
    return pltpu.make_async_remote_copy(
        part.at[(me + k) % n], got.at[k], sems[0].at[k], sems[1].at[k],
        device_id=place(k), device_id_type=MESH)


def gather_copy(whole, sems, k):
    n, me, place = everyone()
    return pltpu.make_async_remote_copy(
        whole.at[me], whole.at[me], sems[2].at[k], sems[3].at[k],
        device_id=place(k), device_id_type=MESH)


def over_peers(act):
    def step(k, _):
        act(k)
        return 0

    lax.fori_loop(1, everyone()[0], step, 0)


def kernel(d2, p1, inp, w1, w2, gin, first, second, e2, e1, t2, t1, acc, faces_out, faces_in,
           edge, part, got, whole, send, recv, *sems, scale):
    ny, nx, ch, nz = d2.shape
    n, me, place = everyone()
    clear_halo(e2)
    clear_halo(e1)
    faces_in[...] = jnp.zeros(faces_in.shape, BF)
    barrier = pltpu.get_barrier_semaphore()

    def greet(k, _):
        pl.semaphore_signal(barrier, inc=1, device_id=place(k), device_id_type=MESH)
        return 0

    lax.fori_loop(1, n, greet, 0)
    e2[pl.ds(1, ny), 1, pl.ds(1, nx)] = d2[...]
    part[...] = jnp.zeros(part.shape, F32)
    edge[...] = jnp.zeros(edge.shape, F32)
    banded(t2, w2, nx)
    pl.semaphore_wait(barrier, n - 1)
    begin, finish = exchange(0, e2, faces_out, faces_in, edge, send, recv)
    begin()
    banded(t1, w1, nx)
    finish()

    def masked(y, value):
        keep = p1[y].reshape(nx * ch, nz).astype(F32) > 0
        e1[y + 1, 1, pl.ds(1, nx)] = jnp.where(keep, value, 0.0).astype(BF).reshape(nx, ch, nz)

    conv(e2, t2, masked, 0, ny // 4)
    begin, finish = exchange(1, e1, faces_out, faces_in, edge, send, recv)
    begin()
    gram(e2, p1, True, acc, part, 1)
    finish()
    gram(e1, inp, False, acc, part, 0)

    def rounded(y, value):
        gin[y] = value.astype(BF).reshape(nx, ch, nz)

    over_peers(lambda k: scatter_copy(part, got, sems, k).start())
    conv(e1, t1, rounded, 0, ny // 8)
    over_peers(lambda k: scatter_copy(part, got, sems, k).wait())
    total = lax.fori_loop(1, n, lambda k, t: t + got[k], part[me])
    whole[me] = (total * scale).astype(BF)
    over_peers(lambda k: gather_copy(whole, sems, k).start())
    conv(e1, t1, rounded, ny // 8, ny // 4)
    over_peers(lambda k: gather_copy(whole, sems, k).wait())
    per = part.shape[1]
    for which, out in enumerate((first, second)):
        for m in range(9):
            for ra in range(3):
                q = (which * 9 + m) * 3 + ra
                lane = q % 4 * ch
                for h in range(ch // 16):
                    block = q // 4 * (ch // 16) + h
                    value = whole[block // per, block % per].astype(F32)
                    out[(2 - ra) * 9 + 8 - m, 16 * h:16 * h + 16, :] = value[:, lane:lane + ch]


def local(inputs, pre_first, pre_second, cotangent, weight_first, weight_second):
    ch, nx, ny, nz = inputs.shape
    cells = nx * ny * nz * lax.axis_size("gx") * lax.axis_size("gy") * lax.axis_size("gz")
    scale = 1.0 / math.sqrt(cells)
    order = (2, 1, 0, 3)
    delta_two = jnp.where(pre_second > 0, cotangent, jnp.zeros_like(cotangent))
    d2, p1, inp = (jnp.transpose(v, order) for v in (delta_two, pre_first, inputs))
    vmem = pl.BlockSpec(memory_space=pltpu.VMEM)
    depth = 9 * (nx + 2) * ch
    brick = (ny + 2, 3, nx + 2, ch, nz)
    n = lax.axis_size("gx") * lax.axis_size("gy") * lax.axis_size("gz")
    per = -(-(-(-2 * 27 // 4) * (ch // 16)) // n)
    gin, first, second = pl.pallas_call(
        functools.partial(kernel, scale=scale),
        out_shape=(jax.ShapeDtypeStruct((ny, nx, ch, nz), BF),
                   jax.ShapeDtypeStruct(weight_first.shape, F32),
                   jax.ShapeDtypeStruct(weight_second.shape, F32)),
        in_specs=[vmem] * 5,
        out_specs=(vmem,) * 3,
        scratch_shapes=[
            pltpu.VMEM(brick, BF),
            pltpu.VMEM(brick, BF),
            pltpu.VMEM((nx * ch, depth), BF),
            pltpu.VMEM((nx * ch, depth), BF),
            pltpu.VMEM((nx * ch, depth), F32),
            pltpu.VMEM((2, 2, ny, nx * ch), BF),
            pltpu.VMEM((2, 2, 9, ny, nx * ch), BF),
            pltpu.VMEM((nz, 256), F32),
            pltpu.VMEM((n, per, 16, 128), F32),
            pltpu.VMEM((n, per, 16, 128), F32),
            pltpu.VMEM((n, per, 16, 128), BF),
            pltpu.SemaphoreType.DMA((2, 26)),
            pltpu.SemaphoreType.DMA((2, 26)),
        ] + [pltpu.SemaphoreType.DMA((n,))] * 4,
        compiler_params=pltpu.CompilerParams(
            collective_id=0, has_side_effects=True, vmem_limit_bytes=48 * 2**20),
    )(d2, p1, inp, weight_first, weight_second)
    return jnp.transpose(gin, order), first, second


def solution(mesh):
    cells = P(None, "gx", "gy", "gz")
    return jax.shard_map(local, mesh=mesh, in_specs=(cells,) * 4 + (P(), P()),
                         out_specs=(cells, P(), P()), check_vma=False)
```

```python
import functools
import math

import jax
import jax.numpy as jnp
from jax import lax
from jax.experimental import pallas as pl
from jax.experimental.pallas import tpu as pltpu
from jax.sharding import PartitionSpec as P

MESH = pl.DeviceIdType.MESH
BF = jnp.bfloat16
F32 = jnp.float32


DIRECTIONS = [(dx, dy, dz) for dz in (0, 1, -1) for dx in (0, 1, -1) for dy in (0, 1, -1)
              if (dx, dy, dz) != (0, 0, 0)]


def near(direction, sign):
    exists, place = None, []
    for axis, d in zip(("gx", "gy", "gz"), direction):
        me, n = lax.axis_index(axis), lax.axis_size(axis)
        if d:
            there = me + sign * d
            ok = (there >= 0) & (there < n)
            exists = ok if exists is None else exists & ok
            me = jnp.clip(there, 0, n - 1)
        place.append(me)
    return exists, tuple(place)


def clear_halo(e):
    rows, _, cols, ch, nz = e.shape
    for y in (0, rows - 1):
        e[y, 1] = jnp.zeros((cols, ch, nz), BF)
    for x in (0, cols - 1):
        e[pl.ds(1, rows - 2), 1, x] = jnp.zeros((rows - 2, ch, nz), BF)


def exchange(k, e, faces_out, faces_in, edge, send, recv):
    rows, _, cols, ch, nz = e.shape
    nx, ny, flat = cols - 2, rows - 2, cols * ch

    def ends(d, n):
        if d == 0:
            return pl.ds(1, n), pl.ds(1, n)
        return (n, 0) if d > 0 else (1, n + 1)

    def copy(i):
        dx, dy, dz = DIRECTIONS[i]
        if dz == 0:
            (sx, tx), (sy, ty) = ends(dx, nx), ends(dy, ny)
            src, dst = e.at[sy, 1, sx], e.at[ty, 1, tx]
        else:
            side = 0 if dz > 0 else 1
            src = faces_out.at[k, side]
            dst = faces_in.at[k, side, (dx + 1) * 3 + dy + 1]
        exists, place = near(DIRECTIONS[i], 1)
        return exists, pltpu.make_async_remote_copy(
            src, dst, send.at[k, i], recv.at[k, i], device_id=place, device_id_type=MESH)

    def start(picked):
        for i in picked:
            exists, one = copy(i)
            pl.when(exists)(one.start)

    def begin():
        start(range(8))
        r = lax.broadcasted_iota(jnp.int32, (2 * ny, 2 * nz), 0)
        lane = lax.broadcasted_iota(jnp.int32, (2 * ny, 2 * nz), 1)
        total = jnp.zeros((2 * ny, nx * ch), F32)
        for y in range(0, ny, 2):
            pick = (((r == y) & (lane == nz - 1)) | ((r == y + ny) & (lane == 0))
                    | ((r == y + 1) & (lane == 2 * nz - 1)) | ((r == y + 1 + ny) & (lane == nz)))
            planes = jnp.concatenate(
                [e[y + 1 + j, 1, pl.ds(1, nx)].reshape(nx * ch, nz) for j in (0, 1)], 1)
            total = total + lax.dot_general(
                jnp.where(pick, 1.0, 0.0).astype(BF), planes,
                (((1,), (1,)), ((), ())), preferred_element_type=F32)
        faces_out[k, 0] = total[:ny].astype(BF)
        faces_out[k, 1] = total[ny:].astype(BF)
        start(range(8, 26))

    def finish():
        for i in range(26):
            exists, one = copy(i)
            pl.when(exists)(one.wait_send)
            came, _ = near(DIRECTIONS[i], -1)
            pl.when(came)(one.wait_recv)

        kk = lax.broadcasted_iota(jnp.int32, (2 * nz, 2 * nz), 0)
        nn = lax.broadcasted_iota(jnp.int32, (2 * nz, 2 * nz), 1)
        own = kk < nz
        left = (nn < nz) & ((own & (kk == nn - 1))
                            | ((nn == 0) & (kk >= nz) & (kk < nz + 32)))
        right = (nn >= nz) & ((own & (kk == nn - nz + 1))
                              | ((nn == 2 * nz - 1) & (kk >= nz + 32) & (kk < nz + 64)))
        shift = jnp.where(left | right, 1.0, 0.0).astype(BF)
        for side in (0, 1):
            for dx in (-1, 0, 1):
                for dy in (-1, 0, 1):
                    face = faces_in[k, side, (dx + 1) * 3 + dy + 1].astype(F32)
                    at = 32 * side
                    if dy == 0:
                        ys, yt = slice(0, ny), slice(at + 1, at + 1 + ny)
                    elif dy > 0:
                        ys, yt = slice(ny - 1, ny), slice(at, at + 1)
                    else:
                        ys, yt = slice(0, 1), slice(at + ny + 1, at + ny + 2)
                    if dx == 0:
                        xs, xt = slice(0, nx * ch), slice(ch, ch + nx * ch)
                    elif dx > 0:
                        xs, xt = slice((nx - 1) * ch, nx * ch), slice(0, ch)
                    else:
                        xs, xt = slice(0, ch), slice((nx + 1) * ch, (nx + 2) * ch)
                    edge[yt, xt] = face[ys, xs]
        columns = edge[...].T[:flat]
        lane = lax.broadcasted_iota(jnp.int32, (flat, nz), 1)

        def step(j, _):
            y = 3 * j
            mine = jnp.concatenate(
                [jnp.where((lane == y + i) | (lane == y + i + 32), columns, 0.0).astype(BF)
                 for i in range(3)], 0)
            planes = e[pl.ds(y, 3), 1].reshape(3 * flat, nz)
            out = jnp.dot(jnp.concatenate([planes, mine], 1), shift,
                          preferred_element_type=F32).astype(BF)
            e[pl.ds(y, 3), 0] = out[:, :nz].reshape(3, cols, ch, nz)
            e[pl.ds(y, 3), 2] = out[:, nz:].reshape(3, cols, ch, nz)
            return 0

        lax.fori_loop(0, rows // 3, step, 0, unroll=2)

    return begin, finish


def banded(t_ref, w_ref, nx):
    ch = w_ref.shape[1]
    t_ref[...] = jnp.zeros(t_ref.shape, BF)
    for x in range(nx):
        for tap in range(27):
            ra, rb, rc = 2 - tap // 9, 2 - tap // 3 % 3, 2 - tap % 3
            col = ((rb * 3 + rc) * (nx + 2) + x + ra) * ch
            t_ref[x * ch:(x + 1) * ch, col:col + ch] = w_ref[tap]


def group(e, y):
    _, three, cols, ch, nz = e.shape
    depth = 3 * three * cols * ch
    return jnp.concatenate([e[pl.ds(y + i, 3)].reshape(depth, nz) for i in range(4)], 1)


def conv(e, t_ref, sink, begin, end):
    nz = e.shape[-1]

    def step(j, _):
        y = 4 * j
        out = jnp.dot(t_ref[...], group(e, y), preferred_element_type=F32)
        for i in range(4):
            sink(y + i, out[:, i * nz:(i + 1) * nz])
        return 0

    lax.fori_loop(begin, end, step, 0, unroll=True)


def gram(e, a_ref, relu, acc, part, which):
    per = part.shape[1]
    ny, nx, ch, nz = a_ref.shape
    acc[...] = jnp.zeros(acc.shape, F32)

    def step(j, _):
        y = 4 * j
        a = jnp.concatenate([a_ref[y + i].reshape(nx * ch, nz) for i in range(4)], 1)
        if relu:
            a = jnp.maximum(a, jnp.zeros_like(a))
        acc[...] += lax.dot_general(a, group(e, y), (((1,), (1,)), ((), ())),
                                    preferred_element_type=F32)
        return 0

    lax.fori_loop(0, ny // 4, step, 0, unroll=True)
    for m in range(9):
        base = m * (nx + 2) * ch
        total = acc[0:ch, base:base + 3 * ch]
        for x in range(1, nx):
            total = total + acc[x * ch:(x + 1) * ch, base + x * ch:base + (x + 3) * ch]
        for ra in range(3):
            q = (which * 9 + m) * 3 + ra
            lane = q % 4 * ch
            for h in range(ch // 16):
                block = q // 4 * (ch // 16) + h
                part[block // per, block % per, :, lane:lane + ch] = (
                    total[16 * h:16 * h + 16, ra * ch:(ra + 1) * ch])


def everyone():
    ny, nz = lax.axis_size("gy"), lax.axis_size("gz")
    n = lax.axis_size("gx") * ny * nz
    me = (lax.axis_index("gx") * ny + lax.axis_index("gy")) * nz + lax.axis_index("gz")

    def place(k):
        p = (me + k) % n
        return (p // (ny * nz), p // nz % ny, p % nz)

    return n, me, place


def scatter_copy(part, got, sems, k):
    n, me, place = everyone()
    return pltpu.make_async_remote_copy(
        part.at[(me + k) % n], got.at[k], sems[0].at[k], sems[1].at[k],
        device_id=place(k), device_id_type=MESH)


def gather_copy(whole, sems, k):
    n, me, place = everyone()
    return pltpu.make_async_remote_copy(
        whole.at[me], whole.at[me], sems[2].at[k], sems[3].at[k],
        device_id=place(k), device_id_type=MESH)


def over_peers(act):
    def step(k, _):
        act(k)
        return 0

    lax.fori_loop(1, everyone()[0], step, 0)


def kernel(d2, p1, inp, w1, w2, gin, first, second, e2, e1, t2, t1, acc, faces_out, faces_in,
           edge, part, got, whole, send, recv, *sems, scale):
    ny, nx, ch, nz = d2.shape
    n, me, place = everyone()
    clear_halo(e2)
    clear_halo(e1)
    faces_in[...] = jnp.zeros(faces_in.shape, BF)
    barrier = pltpu.get_barrier_semaphore()

    def greet(k, _):
        pl.semaphore_signal(barrier, inc=1, device_id=place(k), device_id_type=MESH)
        return 0

    lax.fori_loop(1, n, greet, 0)
    e2[pl.ds(1, ny), 1, pl.ds(1, nx)] = d2[...]
    part[...] = jnp.zeros(part.shape, F32)
    edge[...] = jnp.zeros(edge.shape, F32)
    banded(t2, w2, nx)
    pl.semaphore_wait(barrier, n - 1)
    begin, finish = exchange(0, e2, faces_out, faces_in, edge, send, recv)
    begin()
    banded(t1, w1, nx)
    finish()

    def masked(y, value):
        keep = p1[y].reshape(nx * ch, nz).astype(F32) > 0
        e1[y + 1, 1, pl.ds(1, nx)] = jnp.where(keep, value, 0.0).astype(BF).reshape(nx, ch, nz)

    conv(e2, t2, masked, 0, ny // 4)
    begin, finish = exchange(1, e1, faces_out, faces_in, edge, send, recv)
    begin()
    gram(e2, p1, True, acc, part, 1)
    finish()
    gram(e1, inp, False, acc, part, 0)

    def rounded(y, value):
        gin[y] = value.astype(BF).reshape(nx, ch, nz)

    over_peers(lambda k: scatter_copy(part, got, sems, k).start())
    conv(e1, t1, rounded, 0, ny // 8)
    over_peers(lambda k: scatter_copy(part, got, sems, k).wait())
    total = part[me] + jnp.sum(got[1:], axis=0)
    whole[me] = (total * scale).astype(BF)
    over_peers(lambda k: gather_copy(whole, sems, k).start())
    conv(e1, t1, rounded, ny // 8, ny // 4)
    over_peers(lambda k: gather_copy(whole, sems, k).wait())
    per = part.shape[1]
    for which, out in enumerate((first, second)):
        for m in range(9):
            for ra in range(3):
                q = (which * 9 + m) * 3 + ra
                lane = q % 4 * ch
                for h in range(ch // 16):
                    block = q // 4 * (ch // 16) + h
                    value = whole[block // per, block % per].astype(F32)
                    out[(2 - ra) * 9 + 8 - m, 16 * h:16 * h + 16, :] = value[:, lane:lane + ch]


def local(inputs, pre_first, pre_second, cotangent, weight_first, weight_second):
    ch, nx, ny, nz = inputs.shape
    cells = nx * ny * nz * lax.axis_size("gx") * lax.axis_size("gy") * lax.axis_size("gz")
    scale = 1.0 / math.sqrt(cells)
    order = (2, 1, 0, 3)
    delta_two = jnp.where(pre_second > 0, cotangent, jnp.zeros_like(cotangent))
    d2, p1, inp = (jnp.transpose(v, order) for v in (delta_two, pre_first, inputs))
    vmem = pl.BlockSpec(memory_space=pltpu.VMEM)
    depth = 9 * (nx + 2) * ch
    brick = (ny + 2, 3, nx + 2, ch, nz)
    n = lax.axis_size("gx") * lax.axis_size("gy") * lax.axis_size("gz")
    per = -(-(-(-2 * 27 // 4) * (ch // 16)) // n)
    gin, first, second = pl.pallas_call(
        functools.partial(kernel, scale=scale),
        out_shape=(jax.ShapeDtypeStruct((ny, nx, ch, nz), BF),
                   jax.ShapeDtypeStruct(weight_first.shape, F32),
                   jax.ShapeDtypeStruct(weight_second.shape, F32)),
        in_specs=[vmem] * 5,
        out_specs=(vmem,) * 3,
        scratch_shapes=[
            pltpu.VMEM(brick, BF),
            pltpu.VMEM(brick, BF),
            pltpu.VMEM((nx * ch, depth), BF),
            pltpu.VMEM((nx * ch, depth), BF),
            pltpu.VMEM((nx * ch, depth), F32),
            pltpu.VMEM((2, 2, ny, nx * ch), BF),
            pltpu.VMEM((2, 2, 9, ny, nx * ch), BF),
            pltpu.VMEM((nz, 256), F32),
            pltpu.VMEM((n, per, 16, 128), F32),
            pltpu.VMEM((n, per, 16, 128), F32),
            pltpu.VMEM((n, per, 16, 128), BF),
            pltpu.SemaphoreType.DMA((2, 26)),
            pltpu.SemaphoreType.DMA((2, 26)),
        ] + [pltpu.SemaphoreType.DMA((n,))] * 4,
        compiler_params=pltpu.CompilerParams(
            collective_id=0, has_side_effects=True, vmem_limit_bytes=48 * 2**20),
    )(d2, p1, inp, weight_first, weight_second)
    return jnp.transpose(gin, order), first, second


def solution(mesh):
    cells = P(None, "gx", "gy", "gz")
    return jax.shard_map(local, mesh=mesh, in_specs=(cells,) * 4 + (P(), P()),
                         out_specs=(cells, P(), P()), check_vma=False)
```
